128 devices in a mesh: dp: 2 (over y_lo), row: 16 (over y_hi, x, core), col: 4 (over z).
Axes of the slice: x: 4, y: 4 (y_hi: 2, y_lo: 2; y = y_hi * 2 + y_lo), z: 4, core: 2. Of those that a mesh axis runs over, the one named last changes fastest.
Arguments:
- tokens: bfloat16 [4096, 6144], P(('dp', 'col'), 'row'), may hold values from -6 to 6
- weight: bfloat16 [6144, 24576], P(('dp', 'col'), 'row'), may hold values from -0.078125 to 0.078125
- out_grad: bfloat16 [4096, 24576], P(('dp', 'col'), 'row'), may hold values from -6 to 6
Outputs:
- activated: bfloat16 [4096, 24576], P(('dp', 'col'), 'row')
- token_grad: bfloat16 [4096, 6144], P(('dp', 'col'), 'row')
- weight_grad: bfloat16 [6144, 24576], P(('dp', 'col'), 'row')
The draws below stay inside these ranges and needn't reach their ends.
All inputs are finite; a program needn't handle non-finite values.
Results may differ from the reference program's by a relative error of at most 0.018.
Values may be sent and summed in bfloat16 or wider, within the bound.
No kernel may reach another device: no remote copies, remote signals or barrier semaphores. Data moves between devices by JAX's collectives and lax.ppermute only.
A program may use at most 128 MiB of HBM per device.

```python
import jax
import jax.numpy as jnp
from jax import lax

D = 6144
FF = 24576
TOKENS = 4096
N_DP = 2
N_ROW = 16
N_COL = 4


def block_levels(own_key, dims, pieces, least, top_value):
    def one(axis_at, blocks):
        draws = jax.random.uniform(jax.random.fold_in(jax.random.fold_in(own_key, 6), axis_at), (blocks,), jnp.float32, least / len(pieces), top_value / len(pieces))
        return jnp.repeat(jnp.exp(draws), dims[axis_at] // blocks).reshape((-1,) + (1,) * (len(dims) - axis_at - 1))

    level = one(*pieces[0])
    for cut in pieces[1:]:
        level = level * one(*cut)
    return level


def gaussian(stream_key, shape, spread, limit, pieces=(), held_as=jnp.bfloat16):
    array = spread * jax.random.normal(stream_key, shape, jnp.float32)
    if pieces:
        array = array * block_levels(stream_key, shape, pieces, -0.22, 0.18)
    return jnp.clip(array, -limit, limit).astype(held_as)


def setup_inputs(seed: int = 0) -> dict:
    arg_keys = jax.random.split(jax.random.key(seed), 4)
    tokens = gaussian(arg_keys[0], (TOKENS, D), 1.0, 6.0, ((0, 8), (1, 16)))
    weight = gaussian(arg_keys[1], (D, FF), D ** -0.5, 0.078125, ((0, 8), (1, 16)))
    out_grad = gaussian(arg_keys[2], (TOKENS, FF), 1.0, 6.0, ((0, 8), (1, 16)))
    return {"tokens": tokens, "weight": weight, "out_grad": out_grad}


def gelu_tanh(values_in):
    return jax.nn.gelu(values_in, approximate=True)

def reference(tokens, weight, out_grad):
    pre_act = jnp.dot(tokens, weight, preferred_element_type=jnp.float32)
    activated = gelu_tanh(pre_act).astype(jnp.bfloat16)
    _, pullback = jax.vjp(gelu_tanh, pre_act)
    slope_grad, = pullback(out_grad.astype(jnp.float32))
    pre_grad = slope_grad.astype(jnp.bfloat16)
    block_cols = FF // N_ROW
    grad_blocks = pre_grad.reshape(TOKENS, N_ROW, block_cols).transpose(1, 0, 2)
    weight_blocks = weight.reshape(D, N_ROW, block_cols).transpose(1, 0, 2)

    def add_token_part(running, operands):
        grad_block, weight_block = operands
        product = lax.dot_general(grad_block.astype(jnp.float32), weight_block.astype(jnp.float32), (((1,), (1,)), ((), ())), preferred_element_type=jnp.float32)
        return (running + product.astype(jnp.bfloat16).astype(jnp.float32), None)
    token_sum, _ = lax.scan(add_token_part, jnp.zeros((TOKENS, D), jnp.float32), (grad_blocks, weight_blocks))
    groups = N_DP * N_COL
    group_tokens = tokens.reshape(groups, TOKENS // groups, D)
    group_grads = pre_grad.reshape(groups, TOKENS // groups, FF)

    def add_weight_part(running, operands):
        token_group, grad_group = operands
        product = lax.dot_general(token_group.astype(jnp.float32), grad_group.astype(jnp.float32), (((0,), (0,)), ((), ())), preferred_element_type=jnp.float32)
        return (running + product.astype(jnp.bfloat16).astype(jnp.float32), None)
    weight_sum, _ = lax.scan(add_weight_part, jnp.zeros((D, FF), jnp.float32), (group_tokens, group_grads))
    return (activated, token_sum.astype(jnp.bfloat16), weight_sum.astype(jnp.bfloat16))
```

```python
import jax
import jax.numpy as jnp
from jax import lax
from jax.experimental import pallas as pl
from jax.experimental.pallas import tpu as pltpu
from jax.sharding import PartitionSpec as P

BF, F32 = jnp.bfloat16, jnp.float32
TOK_CUTS = (1, 1)
FF_CUTS = (1, 1)


def gelu_tanh(values_in):
    return jax.nn.gelu(values_in, approximate=True)


def activate(pre_act, out_grad):
    activated, pullback = jax.vjp(gelu_tanh, pre_act)
    (slope_grad,) = pullback(out_grad.astype(F32))
    return activated.astype(BF), slope_grad.astype(BF)


class Steps:
    def __init__(self):
        self.mark = None

    def __call__(self, *values):
        held = values if self.mark is None else (*values, self.mark)
        held = lax.optimization_barrier(held)
        self.mark = held[0]
        return held[: len(values)]


def swap_dp(value):
    return lax.ppermute(value, "dp", [(0, 1), (1, 0)])


def shift_col(value, step):
    return lax.ppermute(value, "col", [(i, (i + step) % 4) for i in range(4)])


def row_of(high, along_x, core):
    return (high * 4 + along_x) * 2 + core


def shift_x(value, step):
    pairs = [
        (row_of(h, x, c), row_of(h, (x + step) % 4, c))
        for h in range(2) for x in range(4) for c in range(2)
    ]
    return lax.ppermute(value, "row", pairs)


def swap_core(value):
    return lax.ppermute(value, "row", [(i, i ^ 1) for i in range(16)])


def turn(value, flip, back=False):
    pairs = [
        (row_of(h, x, c) * 4 + z, row_of(h ^ flip, (x + z) % 4, c) * 4 + x)
        for h in range(2) for x in range(4) for c in range(2) for z in range(4)
    ]
    return lax.ppermute(value, ("row", "col"), [p[::-1] for p in pairs] if back else pairs)


def join_kernel(place, line, mate, own, other):
    _, rows, width = line.shape
    half = width // 2

    def put(first, second):
        for k in range(4):
            j = (k + place[0]) % 4
            at = slice(k * rows, (k + 1) * rows)
            one, two = first[j], second[j]
            own[at, :half], own[at, half:] = one[:, :half], two[:, :half]
            other[at, :half], other[at, half:] = one[:, half:], two[:, half:]

    @pl.when(place[1] == 0)
    def _():
        put(line, mate)

    @pl.when(place[1] == 1)
    def _():
        put(mate, line)


def join_cores(place, line, mate):
    _, rows, width = line.shape
    vmem = pl.BlockSpec(memory_space=pltpu.VMEM)
    return pl.pallas_call(
        join_kernel,
        in_specs=[pl.BlockSpec(memory_space=pltpu.SMEM), vmem, vmem],
        out_specs=[vmem, vmem],
        out_shape=[jax.ShapeDtypeStruct((4 * rows, width), BF)] * 2,
        compiler_params=pltpu.CompilerParams(vmem_limit_bytes=24 * 2**20),
        cost_estimate=pl.CostEstimate(flops=0, bytes_accessed=4 * line.size * 2, transcendentals=0),
    )(place, line, mate)


def part_kernel(place, own, other, mine, theirs):
    _, rows, width = mine.shape
    half = width // 2

    def put(first, second):
        for k in range(4):
            j = (k + place[0]) % 4
            at = slice(k * rows, (k + 1) * rows)
            one, two = own[at], other[at]
            first[j] = jnp.concatenate([one[:, :half], two[:, :half]], axis=1)
            second[j] = jnp.concatenate([one[:, half:], two[:, half:]], axis=1)

    @pl.when(place[1] == 0)
    def _():
        put(mine, theirs)

    @pl.when(place[1] == 1)
    def _():
        put(theirs, mine)


def part_cores(place, own, other):
    rows, width = own.shape[0] // 4, own.shape[1]
    vmem = pl.BlockSpec(memory_space=pltpu.VMEM)
    return pl.pallas_call(
        part_kernel,
        in_specs=[pl.BlockSpec(memory_space=pltpu.SMEM), vmem, vmem],
        out_specs=[vmem, vmem],
        out_shape=[jax.ShapeDtypeStruct((4, rows, width), BF)] * 2,
        compiler_params=pltpu.CompilerParams(vmem_limit_bytes=24 * 2**20),
        cost_estimate=pl.CostEstimate(flops=0, bytes_accessed=4 * own.size * 2, transcendentals=0),
    )(place, own, other)


def cuts_of(size, cuts):
    unit = size // sum(cuts)
    ends = [0]
    for c in cuts:
        ends.append(ends[-1] + c * unit)
    return list(zip(ends[:-1], ends[1:]))


def dot(a, b, over_a, over_b):
    return lax.dot_general(a, b, (((over_a,), (over_b,)), ((), ())), preferred_element_type=F32)


def pick(straight, one, two):
    return jnp.where(straight, one, two), jnp.where(straight, two, one)


def reduce_first(part):
    rows = part.shape[0] // 4
    far = part[2 * rows:3 * rows]
    return shift_col(far[:rows // 2], 1), shift_col(far[rows // 2:], -1)


def reduce_second(part, up, down):
    rows = part.shape[0] // 4
    half = rows // 2
    following, last = part[rows:2 * rows], part[3 * rows:]
    following = jnp.concatenate([(following[:half].astype(F32) + up.astype(F32)).astype(BF), following[half:]])
    last = jnp.concatenate([last[:half], (last[half:].astype(F32) + down.astype(F32)).astype(BF)])
    return shift_col(following, 1), shift_col(last, -1)


def spread_first(grad):
    return shift_col(grad, 1), shift_col(grad, -1)


def spread_second(last, following):
    half = last.shape[0] // 2
    return shift_col(last[:half], 1), shift_col(following[half:], -1)


def local(tokens, weight, out_grad):
    row, z = lax.axis_index("row"), lax.axis_index("col")
    straight = row // 8 == lax.axis_index("dp")
    x, core = row // 2 % 4, row % 2
    place = jnp.stack([(2 * z - x + 8) % 4, core]).astype(jnp.int32)
    t_cuts, f_cuts = cuts_of(tokens.shape[0], TOK_CUTS), cuts_of(weight.shape[1], FF_CUTS)
    step = Steps()
    chunks = ((0, 0), (0, 1), (1, 1), (1, 0))

    w_own = [weight[:, a:b] for a, b in f_cuts]
    w_mate, tok, act, grads = [None] * 2, [None] * 2, {}, {}
    dx_out, dw_out = [None] * 2, [None] * 2

    def turn_tokens(part):
        return turn(part, 0), turn(part, 1)

    def block_of(same, flipped):
        return jnp.concatenate(pick(straight, same, flipped), axis=1)

    def spread_x(block):
        return shift_x(block, -1), shift_x(block, 2), shift_x(block, 1)

    def forward(i):
        t, f = chunks[i]
        return (dot(tok[t][0], w_own[f], 1, 0) + dot(tok[t][1], w_mate[f], 1, 0)).astype(BF)

    def gelu(i, part, one, two):
        t, f = chunks[i]
        rows = part.shape[0] // 4
        pre_act = part[:rows].astype(F32) + one.astype(F32) + two.astype(F32)
        act[t, f], grad = activate(pre_act, out_grad[slice(*t_cuts[t]), slice(*f_cuts[f])])
        return grad

    def gathered(i, grad, last, following, top, bottom):
        grads[chunks[i]] = jnp.concatenate([grad, following, top, bottom, last])

    def token_part(t):
        back = [sum(dot(grads[t, f], w[f], 1, 1) for f in range(2)).astype(BF) for w in (w_own, w_mate)]
        return part_cores(place, *back)

    def weight_part(f, which):
        return sum(dot(tok[t][which], grads[t, f], 0, 0) for t in range(2))

    def line_sum(mine, got):
        return mine.astype(F32) + got.astype(F32)

    def shift_back(line):
        sent = line.astype(BF)
        return shift_x(sent[1], 1), shift_x(sent[2], 2), shift_x(sent[3], -1)

    def turn_back(line, shifted):
        summed = (line[0] + sum(s.astype(F32) for s in shifted)).astype(BF)
        width = summed.shape[1] // 2
        same, flipped = pick(straight, summed[:, :width], summed[:, width:])
        return turn(same, 0, True), turn(flipped, 1, True)

    def token_out(turned):
        return (turned[0].astype(F32) + turned[1].astype(F32)).astype(BF)

    def weight_out(keep, got):
        return (keep + got.astype(F32)).astype(BF)

    turned = step(*turn_tokens(tokens[slice(*t_cuts[0])]))
    w_mate[0] = swap_dp(w_own[0])
    block = block_of(*turned)
    shifted = spread_x(block)
    *shifted, w_mate[0], w_next, part_next = step(*shifted, w_mate[0], w_own[1], tokens[slice(*t_cuts[1])])
    line = jnp.stack([block, *shifted])
    mate = swap_core(line)
    w_mate[1] = swap_dp(w_next)
    turned = turn_tokens(part_next)
    line, mate = step(line, mate)
    tok[0] = join_cores(place, line, mate)
    p0 = forward(0)
    a0 = reduce_first(p0)
    block = block_of(*step(*turned))
    shifted = spread_x(block)
    b0 = reduce_second(p0, *step(*a0))
    w_mate[1], = step(w_mate[1])
    p1 = forward(1)
    a1 = reduce_first(p1)
    g0 = gelu(0, p0, *step(*b0))
    c0 = spread_first(g0)
    b1 = reduce_second(p1, *step(*a1))
    line = jnp.stack([block, *step(*shifted)])
    mate = swap_core(line)
    c0 = step(*c0)
    d0 = spread_second(*c0)
    line, mate = step(line, mate)
    tok[1] = join_cores(place, line, mate)
    p2 = forward(2)
    a2 = reduce_first(p2)
    g1 = gelu(1, p1, *step(*b1))
    c1 = spread_first(g1)
    d0 = step(*d0)
    gathered(0, g0, *c0, *d0)
    b2 = reduce_second(p2, *step(*a2))
    p3 = forward(3)
    *c1, p3 = step(*c1, p3)
    d1 = spread_second(*c1)
    a3 = reduce_first(p3)
    g2 = gelu(2, p2, *step(*b2))
    c2 = spread_first(g2)
    gathered(1, g1, *c1, *step(*d1))
    mine0, theirs0 = token_part(0)
    b3 = reduce_second(p3, *step(*a3))
    got0 = swap_core(theirs0)
    mine0, got0 = step(mine0, got0)
    line0 = line_sum(mine0, got0)
    back0 = shift_back(line0)
    c2 = step(*c2)
    d2 = spread_second(*c2)
    g3 = gelu(3, p3, *step(*b3))
    c3 = spread_first(g3)
    gathered(2, g2, *c2, *step(*d2))
    sent1 = weight_part(1, 1).astype(BF)
    wgot1 = swap_dp(sent1)
    keep1 = weight_part(1, 0)
    c3 = step(*c3)
    d3 = spread_second(*c3)
    turned0 = turn_back(line0, step(*back0))
    gathered(3, g3, *c3, *step(*d3))
    mine1, theirs1 = token_part(1)
    got1 = swap_core(theirs1)
    mine1, theirs1, w_tail = step(mine1, theirs1, grads[1, 0])
    grads[1, 0] = w_tail
    sent0 = weight_part(0, 1).astype(BF)
    wgot0 = swap_dp(sent0)
    got1, sent0 = step(got1, sent0)
    line1 = line_sum(mine1, got1)
    back1 = shift_back(line1)
    keep0 = weight_part(0, 0)
    wgot1, keep0, *turned0 = step(wgot1, keep0, *turned0)
    dw_out[1] = weight_out(keep1, wgot1)
    dx_out[0] = token_out(turned0)
    turned1 = turn_back(line1, step(*back1))
    wgot0, = step(wgot0)
    dw_out[0] = weight_out(keep0, wgot0)
    dx_out[1] = token_out(step(*turned1))
    activated = jnp.concatenate([jnp.concatenate([act[t, f] for f in range(2)], axis=1) for t in range(2)])
    return activated, jnp.concatenate(dx_out), jnp.concatenate(dw_out, axis=1)


def solution(mesh):
    spec = P(("dp", "col"), "row")
    return jax.shard_map(local, mesh=mesh, in_specs=(spec,) * 3, out_specs=(spec,) * 3, check_vma=False)
```

```python
import jax
import jax.numpy as jnp
from jax import lax
from jax.experimental import pallas as pl
from jax.experimental.pallas import tpu as pltpu
from jax.sharding import PartitionSpec as P

BF, F32 = jnp.bfloat16, jnp.float32
TOK_CUTS = (1, 1)
FF_CUTS = (1, 1)
VMEM = pl.BlockSpec(memory_space=pltpu.VMEM)
SMEM = pl.BlockSpec(memory_space=pltpu.SMEM)


class Steps:
    def __init__(self):
        self.mark = None

    def __call__(self, *values):
        held = values if self.mark is None else (*values, self.mark)
        held = lax.optimization_barrier(held)
        self.mark = held[0]
        return held[: len(values)]


def swap_dp(value):
    return lax.ppermute(value, "dp", [(0, 1), (1, 0)])


def shift_col(value, step):
    return lax.ppermute(value, "col", [(i, (i + step) % 4) for i in range(4)])


def row_of(high, along_x, core):
    return (high * 4 + along_x) * 2 + core


def shift_x(value, step):
    pairs = [
        (row_of(h, x, c), row_of(h, (x + step) % 4, c))
        for h in range(2) for x in range(4) for c in range(2)
    ]
    return lax.ppermute(value, "row", pairs)


def swap_core(value):
    return lax.ppermute(value, "row", [(i, i ^ 1) for i in range(16)])


def move(value, target):
    pairs = []
    for high in range(2):
        for along_x in range(4):
            for core in range(2):
                for z in range(4):
                    to_high, to_x, to_z = target(high, along_x, z)
                    pairs.append((row_of(high, along_x, core) * 4 + z, row_of(to_high, to_x % 4, core) * 4 + to_z % 4))
    return lax.ppermute(value, ("row", "col"), pairs)


def turn(value, flip):
    return move(value, lambda h, x, z: (h ^ flip, x + z + 2 * flip, x))


def turn_back_z(value, flip):
    return move(value, lambda h, x, z: (h ^ flip, x, x - z + 2 * flip))


def turn_back_x(value, flip):
    return move(value, lambda h, x, z: (h, x - z + 2 * flip, z))


def gather_first(own, shift):
    return shift(own, 1), shift(own, -1)


def gather_second(last, following, shift):
    half = last.shape[0] // 2
    return shift(last[:half], 1), shift(following[half:], -1)


def reduce_first(top, bottom, shift):
    return shift(top, 1), shift(bottom, -1)


def reduce_second(following, last, up, down, shift):
    half = up.shape[0]
    following = jnp.concatenate([(following[:half].astype(F32) + up.astype(F32)).astype(BF), following[half:]])
    last = jnp.concatenate([last[:half], (last[half:].astype(F32) + down.astype(F32)).astype(BF)])
    return shift(following, 1), shift(last, -1)


def local_call(kernel, shapes, *args, scalars=0, flops=0):
    return pl.pallas_call(
        kernel,
        in_specs=[SMEM] * scalars + [VMEM] * (len(args) - scalars),
        out_specs=[VMEM] * len(shapes),
        out_shape=[jax.ShapeDtypeStruct(s, BF) for s in shapes],
        compiler_params=pltpu.CompilerParams(vmem_limit_bytes=12 * 2**20),
        cost_estimate=pl.CostEstimate(flops=flops, bytes_accessed=0, transcendentals=0),
    )(*args)


def dot(a, b, over_a, over_b):
    return lax.dot_general(a, b, (((over_a,), (over_b,)), ((), ())), preferred_element_type=F32)


def join_cores(place, lines, mates, slots):
    rows, width = sum(v.shape[0] for v in lines) // 4, lines[0].shape[1]
    side, n = width // 2, len(lines)

    def kernel(place, *refs):
        own, other = refs[-2:]
        first = place[1] == 0
        for line, mate, held in zip(refs[:n], refs[n:-2], slots):
            for i, slot in enumerate(held):
                at = slice(i * rows, (i + 1) * rows)
                mine, theirs = line[at], mate[at]
                left, right = jnp.where(first, mine, theirs), jnp.where(first, theirs, mine)
                for out, turned, cols in ((own, place[2], slice(0, side)), (other, place[3], slice(side, width))):
                    to = pl.ds(pl.multiple_of((slot + turned - place[0] + 4) % 4 * rows, rows), rows)
                    out[to, :side], out[to, side:] = left[:, cols], right[:, cols]

    return local_call(kernel, [(4 * rows, width)] * 2, place, *lines, *mates, scalars=1)


def forward(own, other, w_own, w_mate, cut):
    rows, cols = own.shape[0] // 4, cut[1] - cut[0]
    half = rows // 2

    def kernel(own, other, w_own, w_mate, zero, one, top, bottom, three):
        left, right = w_own[:, slice(*cut)], w_mate[...]
        for k in (2, 1, 3, 0):
            at = slice(k * rows, (k + 1) * rows)
            share = (dot(own[at], left, 1, 0) + dot(other[at], right, 1, 0)).astype(BF)
            if k == 2:
                top[...], bottom[...] = share[:half], share[half:]
            else:
                (zero, one, None, three)[k][...] = share

    full, part = (rows, cols), (half, cols)
    return local_call(kernel, [full, full, part, part, full], own, other, w_own, w_mate)


def activate(share, from_last, from_following, out_grad):
    def kernel(share, one, two, out_grad, activated, pre_grad):
        rows = 32
        for r in range(0, share.shape[0], rows):
            at = slice(r, r + rows)
            v = share[at].astype(F32) + one[at].astype(F32) + two[at].astype(F32)
            scale, cubic = 0.7978845608028654, 0.044715
            square = v * v
            tanh = jnp.tanh(scale * (v + cubic * (v * square)))
            gate = 0.5 * (1.0 + tanh)
            activated[at] = (v * gate).astype(BF)
            slope = gate + 0.5 * v * (1.0 - tanh * tanh) * (scale * (1.0 + 3.0 * cubic * square))
            pre_grad[at] = (out_grad[at].astype(F32) * slope).astype(BF)

    return local_call(kernel, [share.shape] * 2, share, from_last, from_following, out_grad)


def token_part(place, grads, w_own, w_mates, cuts, slots, filler):
    rows, width = grads[0].shape[0] // 4, w_own.shape[0]
    side, n = width // 2, len(grads)

    def kernel(place, *refs):
        grads, w_own, w_mates, mine, theirs = refs[:n], refs[n], refs[n + 1:-2], refs[-2], refs[-1]
        for i, slot in enumerate(slots):
            at, at_other = (pl.ds(pl.multiple_of((slot + s - place[0] + 4) % 4 * rows, rows), rows) for s in (place[2], place[3]))
            own = sum(dot(g[at], w_own[:, slice(*cut)], 1, 1) for g, cut in zip(grads, cuts)).astype(BF)
            other = sum(dot(g[at_other], w[...], 1, 1) for g, w in zip(grads, w_mates)).astype(BF)
            zero = jnp.concatenate([own[:, :side], other[:, :side]], axis=1)
            one = jnp.concatenate([own[:, side:], other[:, side:]], axis=1)
            first = place[1] == 0
            to = slice(i * rows, (i + 1) * rows)
            mine[to], theirs[to] = jnp.where(first, zero, one), jnp.where(first, one, zero)

    shape = (len(slots) * rows, width)
    flops = 4 * shape[0] * w_own.size if filler else 0
    return local_call(kernel, [shape, shape], place, *grads, w_own, *w_mates, scalars=1, flops=flops)


def weight_part(tokens, grads, filler):
    n, width, cols = len(tokens), tokens[0].shape[1], grads[0].shape[1]
    block = min(256, width)

    def kernel(*refs):
        tokens, grads, out = refs[:n], refs[n:-1], refs[-1]
        for c in range(0, width, block):
            out[c:c + block] = sum(dot(t[:, c:c + block], g[...], 0, 0) for t, g in zip(tokens, grads)).astype(BF)

    flops = 2 * n * tokens[0].size * cols if filler else 0
    return local_call(kernel, [(width, cols)], *tokens, *grads, flops=flops)[0]


def add(*values):
    return sum(v.astype(F32) for v in values).astype(BF)


def cuts_of(size, cuts):
    unit = size // sum(cuts)
    ends = [0]
    for c in cuts:
        ends.append(ends[-1] + c * unit)
    return list(zip(ends[:-1], ends[1:]))


def pick(straight, one, two):
    return jnp.where(straight, one, two), jnp.where(straight, two, one)


def local(tokens, weight, out_grad):
    row, z = lax.axis_index("row"), lax.axis_index("col")
    straight = row // 8 == lax.axis_index("dp")
    x, core = row // 2 % 4, row % 2
    place = jnp.stack([(2 * z - x + 8) % 4, core, *pick(straight, 0, 2)]).astype(jnp.int32)
    t_cuts, f_cuts = cuts_of(tokens.shape[0], TOK_CUTS), cuts_of(weight.shape[1], FF_CUTS)
    step = Steps()
    chunks = ((0, 0), (0, 1), (1, 0), (1, 1))
    w_mate, tok, act, grads = [None] * 2, [None] * 2, {}, {}
    parts, acts, pre = {}, {}, {}

    def project(i):
        t, f = chunks[i]
        parts[i] = forward(*tok[t], weight, w_mate[f], f_cuts[f])
        return reduce_first(parts[i][2], parts[i][3], shift_col)

    def reduce_on(i, up, down):
        return reduce_second(parts[i][1], parts[i][4], up, down, shift_col)

    def activate_on(i, one, two):
        t, f = chunks[i]
        act[t, f], pre[i] = activate(parts[i][0], one, two, out_grad[slice(*t_cuts[t]), slice(*f_cuts[f])])
        return gather_first(pre[i], shift_col)

    def gathered(i, last, following, top, bottom):
        grads[chunks[i]] = jnp.concatenate([pre[i], following, top, bottom, last])

    def back(t, slots, filler=False):
        return token_part(place, [grads[t, f] for f in range(2)], weight, w_mate, f_cuts, slots, filler)

    def weight_back(f, which, filler=True):
        return weight_part([tok[t][which] for t in range(2)], [grads[t, f] for t in range(2)], filler)

    def turn_back(summed):
        width = summed.shape[1] // 2
        same, flipped = pick(straight, summed[:, :width], summed[:, width:])
        return turn_back_z(same, 0), turn_back_z(flipped, 1)

    same, flipped = turn(tokens, 0), turn(tokens, 1)
    same, w_first = step(same, weight[:, slice(*f_cuts[0])])
    flipped, = step(flipped)
    w_mate[0] = swap_dp(w_first)
    block = jnp.concatenate(pick(straight, same, flipped), axis=1)
    b0, b1 = block[slice(*t_cuts[0])], block[slice(*t_cuts[1])]
    last, following = step(*gather_first(b0, shift_x))
    far = gather_second(last, following, shift_x)
    three = jnp.concatenate([b0, following, last])
    mate_three = swap_core(three)
    top, bottom, b1, w_next = step(*far, b1, weight[:, slice(*f_cuts[1])])
    far = jnp.concatenate([top, bottom])
    mate_far = swap_core(far)
    w_mate[1] = swap_dp(w_next)
    mate_far, mate_three, w_mate[0] = step(mate_far, mate_three, w_mate[0])
    tok[0] = join_cores(place, (three, far), (mate_three, mate_far), ((0, 1, 3), (2,)))
    a = project(0)
    b1, _ = step(b1, parts[0][0])
    ring = [b1, shift_x(b1, 1)]
    a = reduce_on(0, *step(*a))
    ring[1], = step(ring[1])
    ring.append(shift_x(ring[1], 1))

    a = activate_on(0, *step(*a))
    ring[2], _ = step(ring[2], pre[0])
    ring.append(shift_x(ring[2], 1))
    w_mate[1], = step(w_mate[1])
    b = project(1)
    a0 = step(*a, parts[1][0])[:2]
    a = gather_second(*a0, shift_col)
    ring[3], = step(ring[3])
    line = jnp.concatenate(ring)
    mate = swap_core(line)
    b = reduce_on(1, *step(*b))
    gathered(0, *a0, *step(*a))
    mate, = step(mate)
    tok[1] = join_cores(place, (line,), (mate,), ((0, 3, 2, 1),))
    a = project(2)
    b = activate_on(1, *step(*b, parts[2][0])[:2])
    a = reduce_on(2, *step(*a, pre[1])[:2])
    b0 = step(*b)
    b = gather_second(*b0, shift_col)
    a = activate_on(2, *step(*a))
    gathered(1, *b0, *step(*b, pre[2])[:2])
    b = project(3)
    b = reduce_on(3, *step(*b))
    grads[chunks[1]], = step(grads[chunks[1]])
    mine, theirs = back(0, (0, 1, 2, 3), True)
    got = swap_core(theirs)
    a0 = step(*a, theirs)[:2]
    a = gather_second(*a0, shift_col)
    rows = t_cuts[0][1]
    slots = [slice(k * rows, (k + 1) * rows) for k in range(4)]
    got, = step(got)
    x_sum = shift_x(add(mine[slots[3]], got[slots[3]]), 1)
    b = activate_on(3, *step(*b))
    x_sum, _ = step(x_sum, pre[3])
    x_sum = shift_x(add(mine[slots[2]], got[slots[2]], x_sum), 1)
    gathered(2, *a0, *step(*a))
    sent0 = weight_back(0, 1)
    wgot0 = swap_dp(sent0)
    b0 = step(*b, sent0)[:2]
    b = gather_second(*b0, shift_col)
    x_sum, = step(x_sum)
    x_sum = shift_x(add(mine[slots[1]], got[slots[1]], x_sum), 1)
    keep0 = weight_back(0, 0)

    gathered(3, *b0, *step(*b, keep0)[:2])
    mine1_far, theirs1_far = back(1, (2,))
    got_far = swap_core(theirs1_far)
    grads[chunks[3]], _ = step(grads[chunks[3]], theirs1_far)
    sent1 = weight_back(1, 1, False)
    wgot1 = swap_dp(sent1)
    got_far, grads[chunks[3]], _ = step(got_far, grads[chunks[3]], sent1)
    line = add(mine1_far, got_far)
    half = line.shape[0] // 2
    x_first = reduce_first(line[:half], line[half:], shift_x)
    mine1, theirs1 = back(1, (0, 1, 3))
    got1 = swap_core(theirs1)
    x_sum, wgot0, _ = step(x_sum, wgot0, theirs1)
    sum0 = add(mine[slots[0]], got[slots[0]], x_sum)
    dw_out = [add(keep0, wgot0), None]
    *x_first, got1, tok_keep, _, _ = step(*x_first, got1, tok[1][0], sum0, dw_out[0])
    tok[1] = (tok_keep, tok[1][1])
    line = add(mine1, got1)
    rows = 2 * half
    x_second = reduce_second(line[rows:2 * rows], line[2 * rows:], *x_first, shift_x)
    keep1 = weight_back(1, 0)
    *x_second, wgot1, _ = step(*x_second, wgot1, keep1)
    same, flipped = turn_back(jnp.concatenate([sum0, add(line[:rows], *x_second)]))
    dw_out[1] = add(keep1, wgot1)
    same, flipped, _ = step(same, flipped, dw_out[1])
    dx_out = [add(*step(turn_back_x(same, 0), turn_back_x(flipped, 1)))]
    activated = jnp.concatenate([jnp.concatenate([act[t, f] for f in range(2)], axis=1) for t in range(2)])
    return activated, jnp.concatenate(dx_out), jnp.concatenate(dw_out, axis=1)


def solution(mesh):
    spec = P(("dp", "col"), "row")
    return jax.shard_map(local, mesh=mesh, in_specs=(spec,) * 3, out_specs=(spec,) * 3, check_vma=False)
```

```python
import jax
import jax.numpy as jnp
from jax import lax
from jax.experimental import pallas as pl
from jax.experimental.pallas import tpu as pltpu
from jax.sharding import PartitionSpec as P

BF, F32 = jnp.bfloat16, jnp.float32
TOK_CUTS = (1, 1)
FF_CUTS = (1, 1)
VMEM = pl.BlockSpec(memory_space=pltpu.VMEM)
SMEM = pl.BlockSpec(memory_space=pltpu.SMEM)


class Steps:
    def __init__(self):
        self.mark = None

    def __call__(self, *values):
        held = values if self.mark is None else (*values, self.mark)
        held = lax.optimization_barrier(held)
        self.mark = held[0]
        return held[: len(values)]


def swap_dp(value):
    return lax.ppermute(value, "dp", [(0, 1), (1, 0)])


def shift_col(value, step):
    return lax.ppermute(value, "col", [(i, (i + step) % 4) for i in range(4)])


def row_of(high, along_x, core):
    return (high * 4 + along_x) * 2 + core


def shift_x(value, step):
    pairs = [
        (row_of(h, x, c), row_of(h, (x + step) % 4, c))
        for h in range(2) for x in range(4) for c in range(2)
    ]
    return lax.ppermute(value, "row", pairs)


def swap_core(value):
    return lax.ppermute(value, "row", [(i, i ^ 1) for i in range(16)])


def move(value, target):
    pairs = []
    for high in range(2):
        for along_x in range(4):
            for core in range(2):
                for z in range(4):
                    to_high, to_x, to_z = target(high, along_x, z)
                    pairs.append((row_of(high, along_x, core) * 4 + z, row_of(to_high, to_x % 4, core) * 4 + to_z % 4))
    return lax.ppermute(value, ("row", "col"), pairs)


def turn(value, flip):
    return move(value, lambda h, x, z: (h ^ flip, x + z + 2 * flip, x))


def turn_back_z(value, flip):
    return move(value, lambda h, x, z: (h, x, x - z + 2 * flip))


def turn_back_x(value, flip):
    return move(value, lambda h, x, z: (h ^ flip, x - z + 2 * flip, z))


def gather_first(own, shift):
    return shift(own, 1), shift(own, -1)


def gather_second(last, following, shift):
    half = last.shape[0] // 2
    return shift(last[:half], 1), shift(following[half:], -1)


def reduce_first(top, bottom, shift):
    return shift(top, 1), shift(bottom, -1)


def reduce_second(following, last, up, down, shift):
    half = up.shape[0]
    following = jnp.concatenate([(following[:half].astype(F32) + up.astype(F32)).astype(BF), following[half:]])
    last = jnp.concatenate([last[:half], (last[half:].astype(F32) + down.astype(F32)).astype(BF)])
    return shift(following, 1), shift(last, -1)


def local_call(kernel, shapes, *args, scalars=0, flops=0):
    return pl.pallas_call(
        kernel,
        in_specs=[SMEM] * scalars + [VMEM] * (len(args) - scalars),
        out_specs=[VMEM] * len(shapes),
        out_shape=[jax.ShapeDtypeStruct(s, BF) for s in shapes],
        compiler_params=pltpu.CompilerParams(vmem_limit_bytes=12 * 2**20),
        cost_estimate=pl.CostEstimate(flops=flops, bytes_accessed=0, transcendentals=0),
    )(*args)


def dot(a, b, over_a, over_b):
    return lax.dot_general(a, b, (((over_a,), (over_b,)), ((), ())), preferred_element_type=F32)


def join_cores(place, lines, mates, slots):
    rows, width = sum(v.shape[0] for v in lines) // 4, lines[0].shape[1]
    side, n = width // 2, len(lines)

    def kernel(place, *refs):
        own, other = refs[-2:]
        first = place[1] == 0
        for line, mate, held in zip(refs[:n], refs[n:-2], slots):
            for i, slot in enumerate(held):
                at = slice(i * rows, (i + 1) * rows)
                mine, theirs = line[at], mate[at]
                left, right = jnp.where(first, mine, theirs), jnp.where(first, theirs, mine)
                for out, turned, cols in ((own, place[2], slice(0, side)), (other, place[3], slice(side, width))):
                    to = pl.ds(pl.multiple_of((slot + turned - place[0] + 4) % 4 * rows, rows), rows)
                    out[to, :side], out[to, side:] = left[:, cols], right[:, cols]

    return local_call(kernel, [(4 * rows, width)] * 2, place, *lines, *mates, scalars=1)


def forward(own, other, w_own, w_mate, cut):
    rows, cols = own.shape[0] // 4, cut[1] - cut[0]
    half = rows // 2

    def kernel(own, other, w_own, w_mate, zero, one, top, bottom, three):
        left, right = w_own[:, slice(*cut)], w_mate[...]
        for k in (2, 1, 3, 0):
            at = slice(k * rows, (k + 1) * rows)
            share = (dot(own[at], left, 1, 0) + dot(other[at], right, 1, 0)).astype(BF)
            if k == 2:
                top[...], bottom[...] = share[:half], share[half:]
            else:
                (zero, one, None, three)[k][...] = share

    full, part = (rows, cols), (half, cols)
    return local_call(kernel, [full, full, part, part, full], own, other, w_own, w_mate)


def activate(share, from_last, from_following, out_grad):
    def kernel(share, one, two, out_grad, activated, pre_grad):
        rows = 32
        for r in range(0, share.shape[0], rows):
            at = slice(r, r + rows)
            v = share[at].astype(F32) + one[at].astype(F32) + two[at].astype(F32)
            scale, cubic = 0.7978845608028654, 0.044715
            square = v * v
            tanh = jnp.tanh(scale * (v + cubic * (v * square)))
            gate = 0.5 * (1.0 + tanh)
            activated[at] = (v * gate).astype(BF)
            slope = gate + 0.5 * v * (1.0 - tanh * tanh) * (scale * (1.0 + 3.0 * cubic * square))
            pre_grad[at] = (out_grad[at].astype(F32) * slope).astype(BF)

    return local_call(kernel, [share.shape] * 2, share, from_last, from_following, out_grad)


def token_part(place, grads, w_own, w_mates, cuts, slots, filler):
    rows, width = grads[0].shape[0] // 4, w_own.shape[0]
    side, n = width // 2, len(grads)

    def kernel(place, *refs):
        grads, w_own, w_mates, mine, theirs = refs[:n], refs[n], refs[n + 1:-2], refs[-2], refs[-1]
        for i, slot in enumerate(slots):
            at, at_other = (pl.ds(pl.multiple_of((slot + s - place[0] + 4) % 4 * rows, rows), rows) for s in (place[2], place[3]))
            own = sum(dot(g[at], w_own[:, slice(*cut)], 1, 1) for g, cut in zip(grads, cuts)).astype(BF)
            other = sum(dot(g[at_other], w[...], 1, 1) for g, w in zip(grads, w_mates)).astype(BF)
            zero = jnp.concatenate([own[:, :side], other[:, :side]], axis=1)
            one = jnp.concatenate([own[:, side:], other[:, side:]], axis=1)
            first = place[1] == 0
            to = slice(i * rows, (i + 1) * rows)
            mine[to], theirs[to] = jnp.where(first, zero, one), jnp.where(first, one, zero)

    shape = (len(slots) * rows, width)
    flops = 4 * shape[0] * w_own.size if filler else 0
    return local_call(kernel, [shape, shape], place, *grads, w_own, *w_mates, scalars=1, flops=flops)


def weight_part(tokens, grads, cut):
    n, width, cols = len(tokens), tokens[0].shape[1], cut[1] - cut[0]
    block = min(256, width)

    def kernel(*refs):
        tokens, grads, out = refs[:n], refs[n:-1], refs[-1]
        for c in range(0, width, block):
            out[c:c + block] = sum(dot(t[:, c:c + block], g[:, slice(*cut)], 0, 0) for t, g in zip(tokens, grads)).astype(BF)

    return local_call(kernel, [(width, cols)], *tokens, *grads)[0]


def add(*values):
    return sum(v.astype(F32) for v in values).astype(BF)


def cuts_of(size, cuts):
    unit = size // sum(cuts)
    ends = [0]
    for c in cuts:
        ends.append(ends[-1] + c * unit)
    return list(zip(ends[:-1], ends[1:]))


def pick(straight, one, two):
    return jnp.where(straight, one, two), jnp.where(straight, two, one)


def local(tokens, weight, out_grad):
    row, z = lax.axis_index("row"), lax.axis_index("col")
    straight = row // 8 == lax.axis_index("dp")
    x, core = row // 2 % 4, row % 2
    place = jnp.stack([(2 * z - x + 8) % 4, core, *pick(straight, 0, 2)]).astype(jnp.int32)
    t_cuts, f_cuts = cuts_of(tokens.shape[0], TOK_CUTS), cuts_of(weight.shape[1], FF_CUTS)
    step = Steps()
    chunks = ((0, 0), (0, 1), (1, 0), (1, 1))
    w_mate, tok, act, grads = [None] * 2, [None] * 2, {}, {}
    parts, acts, pre = {}, {}, {}

    def project(i):
        t, f = chunks[i]
        parts[i] = forward(*tok[t], weight, w_mate[f], f_cuts[f])
        return reduce_first(parts[i][2], parts[i][3], shift_col)

    def reduce_on(i, up, down):
        return reduce_second(parts[i][1], parts[i][4], up, down, shift_col)

    def activate_on(i, one, two):
        t, f = chunks[i]
        act[t, f], pre[i] = activate(parts[i][0], one, two, out_grad[slice(*t_cuts[t]), slice(*f_cuts[f])])
        return gather_first(pre[i], shift_col)

    def gathered(i, last, following, top, bottom):
        grads[chunks[i]] = jnp.concatenate([pre[i], following, top, bottom, last])

    def back(t, slots, filler=False):
        return token_part(place, [grads[t, f] for f in range(2)], weight, w_mate, f_cuts, slots, filler)

    def weight_back(f, which, part=0, of=1):
        cols = (f_cuts[f][1] - f_cuts[f][0]) // of
        cut = (part * cols, (part + 1) * cols)
        return weight_part([tok[t][which] for t in range(2)], [grads[t, f] for t in range(2)], cut)

    def turn_back(summed):
        width = summed.shape[1] // 2
        same, flipped = pick(straight, summed[:, :width], summed[:, width:])
        return turn_back_z(same, 0), turn_back_z(flipped, 1)

    same, flipped = turn(tokens, 0), turn(tokens, 1)
    same, w_first = step(same, weight[:, slice(*f_cuts[0])])
    flipped, = step(flipped)
    w_mate[0] = swap_dp(w_first)
    block = jnp.concatenate(pick(straight, same, flipped), axis=1)
    b0, b1 = block[slice(*t_cuts[0])], block[slice(*t_cuts[1])]
    last, following = step(*gather_first(b0, shift_x))
    far = gather_second(last, following, shift_x)
    three = jnp.concatenate([b0, following, last])
    mate_three = swap_core(three)
    top, bottom, b1, w_next = step(*far, b1, weight[:, slice(*f_cuts[1])])
    far = jnp.concatenate([top, bottom])
    mate_far = swap_core(far)
    w_mate[1] = swap_dp(w_next)
    mate_far, mate_three, w_mate[0] = step(mate_far, mate_three, w_mate[0])
    tok[0] = join_cores(place, (three, far), (mate_three, mate_far), ((0, 1, 3), (2,)))
    a = project(0)
    b1, _ = step(b1, parts[0][0])
    ring = [b1, shift_x(b1, 1)]
    a = reduce_on(0, *step(*a))
    ring[1], = step(ring[1])
    ring.append(shift_x(ring[1], 1))

    a = activate_on(0, *step(*a))
    ring[2], _ = step(ring[2], pre[0])
    ring.append(shift_x(ring[2], 1))
    w_mate[1], = step(w_mate[1])
    b = project(1)
    a0 = step(*a, parts[1][0])[:2]
    a = gather_second(*a0, shift_col)
    *b, ring[3], top, bottom = step(*b, ring[3], *a)
    b = reduce_on(1, *b)
    line = jnp.concatenate(ring)
    mate = swap_core(line)
    gathered(0, *a0, top, bottom)
    mate, = step(mate)
    tok[1] = join_cores(place, (line,), (mate,), ((0, 3, 2, 1),))
    a = project(2)
    b = activate_on(1, *step(*b, parts[2][0])[:2])
    a = reduce_on(2, *step(*a, pre[1])[:2])
    b0 = step(*b)
    b = gather_second(*b0, shift_col)
    a = activate_on(2, *step(*a))
    gathered(1, *b0, *step(*b, pre[2])[:2])
    b = project(3)
    mine3, theirs = back(0, (3,))
    got3 = swap_core(theirs)
    *b, grads[chunks[1]], _ = step(*b, grads[chunks[1]], theirs)
    b = reduce_on(3, *b)
    mine2, theirs = back(0, (2,))
    got2 = swap_core(theirs)
    *a0, got3, grads[chunks[1]], _ = step(*a, got3, grads[chunks[1]], theirs)
    a = gather_second(*a0, shift_col)
    x_sum = shift_x(add(mine3, got3), 1)
    *b, got2 = step(*b, got2)
    b = activate_on(3, *b)
    mine1, theirs = back(0, (1,))
    got1 = swap_core(theirs)
    *a, x_sum, grads[chunks[1]], _, _ = step(*a, x_sum, grads[chunks[1]], theirs, pre[3])
    gathered(2, *a0, *a)
    x_sum = shift_x(add(mine2, got2, x_sum), 1)
    sent = weight_back(0, 1)
    wgot0 = swap_dp(sent)
    *b0, got1, grads[chunks[2]], _ = step(*b, got1, grads[chunks[2]], sent)
    b = gather_second(*b0, shift_col)
    mine0, theirs = back(0, (0,))
    got0 = swap_core(theirs)
    *b, x_sum, grads[chunks[2]], _ = step(*b, x_sum, grads[chunks[2]], theirs)
    x_sum = shift_x(add(mine1, got1, x_sum), 1)

    gathered(3, *b0, *b)
    mine2, theirs = back(1, (2,))
    got2 = swap_core(theirs)
    grads[chunks[3]], _ = step(grads[chunks[3]], theirs)
    mine, theirs = back(1, (1, 3))
    got = swap_core(theirs)
    got2, grads[chunks[3]], _ = step(got2, grads[chunks[3]], theirs)
    line = add(mine2, got2)
    half = line.shape[0] // 2
    x_first = reduce_first(line[:half], line[half:], shift_x)
    sent = weight_back(1, 1, 0, 2)
    *x_first, got, wgot0, grads[chunks[2]], grads[chunks[3]], sent = step(
        *x_first, got, wgot0, grads[chunks[2]], grads[chunks[3]], sent
    )
    wgot1 = [swap_dp(sent)]
    line = add(mine, got)
    rows = 2 * half
    x_second = reduce_second(line[:rows], line[rows:], *x_first, shift_x)
    mine1, theirs = back(1, (0,))
    got1 = swap_core(theirs)
    sent = weight_back(1, 1, 1, 2)
    keep0 = weight_back(0, 0)
    *x_second, x_sum, got0, got1, wgot1[0], sent, tok_keep, keep0 = step(
        *x_second, x_sum, got0, got1, wgot1[0], sent, tok[1][0], keep0
    )
    wgot1.append(swap_dp(sent))
    sum0, sum1 = add(mine0, got0, x_sum), add(mine1, got1, *x_second)
    same, flipped = turn_back(jnp.concatenate([sum0, sum1]))
    dw_out = [add(keep0, wgot0), None]
    tok[1] = (tok_keep, tok[1][1])
    keep1 = weight_back(1, 0)
    same, flipped, wgot1[1], keep1, _ = step(same, flipped, wgot1[1], keep1, dw_out[0])
    turned = turn_back_x(same, 0), turn_back_x(flipped, 1)
    dw_out[1] = add(keep1, jnp.concatenate(wgot1, axis=1))
    dx_out = [add(*step(*turned, dw_out[1])[:2])]
    activated = jnp.concatenate([jnp.concatenate([act[t, f] for f in range(2)], axis=1) for t in range(2)])
    return activated, jnp.concatenate(dx_out), jnp.concatenate(dw_out, axis=1)


def solution(mesh):
    spec = P(("dp", "col"), "row")
    return jax.shard_map(local, mesh=mesh, in_specs=(spec,) * 3, out_specs=(spec,) * 3, check_vma=False)
```

```python
import jax
import jax.numpy as jnp
from jax import lax
from jax.experimental import pallas as pl
from jax.experimental.pallas import tpu as pltpu
from jax.sharding import PartitionSpec as P

BF, F32 = jnp.bfloat16, jnp.float32
TOK_CUTS = (1, 1)
FF_CUTS = (1, 1)
VMEM = pl.BlockSpec(memory_space=pltpu.VMEM)
SMEM = pl.BlockSpec(memory_space=pltpu.SMEM)


class Steps:
    def __init__(self):
        self.mark = None

    def __call__(self, *values):
        held = values if self.mark is None else (*values, self.mark)
        held = lax.optimization_barrier(held)
        self.mark = held[0]
        return held[: len(values)]


def swap_dp(value):
    return lax.ppermute(value, "dp", [(0, 1), (1, 0)])


def shift_col(value, step):
    return lax.ppermute(value, "col", [(i, (i + step) % 4) for i in range(4)])


def row_of(high, along_x, core):
    return (high * 4 + along_x) * 2 + core


def shift_x(value, step):
    pairs = [
        (row_of(h, x, c), row_of(h, (x + step) % 4, c))
        for h in range(2) for x in range(4) for c in range(2)
    ]
    return lax.ppermute(value, "row", pairs)


def swap_core(value):
    return lax.ppermute(value, "row", [(i, i ^ 1) for i in range(16)])


def move(value, target):
    pairs = []
    for high in range(2):
        for along_x in range(4):
            for core in range(2):
                for z in range(4):
                    to_high, to_x, to_z = target(high, along_x, z)
                    pairs.append((row_of(high, along_x, core) * 4 + z, row_of(to_high, to_x % 4, core) * 4 + to_z % 4))
    return lax.ppermute(value, ("row", "col"), pairs)


def turn(value, flip):
    return move(value, lambda h, x, z: (h ^ flip, x + z + 2 * flip, x))


def turn_back_z(value, flip):
    return move(value, lambda h, x, z: (h, x, x - z + 2 * flip))


def turn_back_x(value, flip):
    return move(value, lambda h, x, z: (h ^ flip, x - z + 2 * flip, z))


def gather_first(own, shift):
    return shift(own, 1), shift(own, -1)


def gather_second(last, following, shift):
    half = last.shape[0] // 2
    return shift(last[:half], 1), shift(following[half:], -1)


def reduce_first(top, bottom, shift):
    return shift(top, 1), shift(bottom, -1)


def reduce_second(following, last, up, down, shift):
    half = up.shape[0]
    following = jnp.concatenate([(following[:half].astype(F32) + up.astype(F32)).astype(BF), following[half:]])
    last = jnp.concatenate([last[:half], (last[half:].astype(F32) + down.astype(F32)).astype(BF)])
    return shift(following, 1), shift(last, -1)


def local_call(kernel, shapes, *args, scalars=0, flops=0):
    return pl.pallas_call(
        kernel,
        in_specs=[SMEM] * scalars + [VMEM] * (len(args) - scalars),
        out_specs=[VMEM] * len(shapes),
        out_shape=[jax.ShapeDtypeStruct(s, BF) for s in shapes],
        compiler_params=pltpu.CompilerParams(vmem_limit_bytes=12 * 2**20),
        cost_estimate=pl.CostEstimate(flops=flops, bytes_accessed=0, transcendentals=0),
    )(*args)


def dot(a, b, over_a, over_b):
    return lax.dot_general(a, b, (((over_a,), (over_b,)), ((), ())), preferred_element_type=F32)


def join_cores(place, lines, mates, slots):
    rows, width = sum(v.shape[0] for v in lines) // 4, lines[0].shape[1]
    side, n = width // 2, len(lines)

    def kernel(place, *refs):
        own, other = refs[-2:]
        first = place[1] == 0
        for line, mate, held in zip(refs[:n], refs[n:-2], slots):
            for i, slot in enumerate(held):
                at = slice(i * rows, (i + 1) * rows)
                mine, theirs = line[at], mate[at]
                left, right = jnp.where(first, mine, theirs), jnp.where(first, theirs, mine)
                for out, turned, cols in ((own, place[2], slice(0, side)), (other, place[3], slice(side, width))):
                    to = pl.ds(pl.multiple_of((slot + turned - place[0] + 4) % 4 * rows, rows), rows)
                    out[to, :side], out[to, side:] = left[:, cols], right[:, cols]

    return local_call(kernel, [(4 * rows, width)] * 2, place, *lines, *mates, scalars=1)


def forward(own, other, w_own, w_mate, cut):
    rows, cols = own.shape[0] // 4, cut[1] - cut[0]
    half = rows // 2

    def kernel(own, other, w_own, w_mate, zero, one, top, bottom, three):
        left, right = w_own[:, slice(*cut)], w_mate[...]
        for k in (2, 1, 3, 0):
            at = slice(k * rows, (k + 1) * rows)
            share = (dot(own[at], left, 1, 0) + dot(other[at], right, 1, 0)).astype(BF)
            if k == 2:
                top[...], bottom[...] = share[:half], share[half:]
            else:
                (zero, one, None, three)[k][...] = share

    full, part = (rows, cols), (half, cols)
    return local_call(kernel, [full, full, part, part, full], own, other, w_own, w_mate)


def activate(share, from_last, from_following, out_grad):
    def kernel(share, one, two, out_grad, activated, pre_grad):
        rows = 32
        for r in range(0, share.shape[0], rows):
            at = slice(r, r + rows)
            v = share[at].astype(F32) + one[at].astype(F32) + two[at].astype(F32)
            scale, cubic = 0.7978845608028654, 0.044715
            square = v * v
            tanh = jnp.tanh(scale * (v + cubic * (v * square)))
            gate = 0.5 * (1.0 + tanh)
            activated[at] = (v * gate).astype(BF)
            slope = gate + 0.5 * v * (1.0 - tanh * tanh) * (scale * (1.0 + 3.0 * cubic * square))
            pre_grad[at] = (out_grad[at].astype(F32) * slope).astype(BF)

    return local_call(kernel, [share.shape] * 2, share, from_last, from_following, out_grad)


def token_part(place, grads, w_own, w_mates, cuts, slots, filler):
    rows, width = grads[0].shape[0] // 4, w_own.shape[0]
    side, n = width // 2, len(grads)

    def kernel(place, *refs):
        grads, w_own, w_mates, mine, theirs = refs[:n], refs[n], refs[n + 1:-2], refs[-2], refs[-1]
        for i, slot in enumerate(slots):
            at, at_other = (pl.ds(pl.multiple_of((slot + s - place[0] + 4) % 4 * rows, rows), rows) for s in (place[2], place[3]))
            own = sum(dot(g[at], w_own[:, slice(*cut)], 1, 1) for g, cut in zip(grads, cuts)).astype(BF)
            other = sum(dot(g[at_other], w[...], 1, 1) for g, w in zip(grads, w_mates)).astype(BF)
            zero = jnp.concatenate([own[:, :side], other[:, :side]], axis=1)
            one = jnp.concatenate([own[:, side:], other[:, side:]], axis=1)
            first = place[1] == 0
            to = slice(i * rows, (i + 1) * rows)
            mine[to], theirs[to] = jnp.where(first, zero, one), jnp.where(first, one, zero)

    shape = (len(slots) * rows, width)
    flops = 4 * shape[0] * w_own.size if filler else 0
    return local_call(kernel, [shape, shape], place, *grads, w_own, *w_mates, scalars=1, flops=flops)


def weight_part(tokens, grads, cut):
    n, width, cols = len(tokens), tokens[0].shape[1], cut[1] - cut[0]
    block = min(256, width)

    def kernel(*refs):
        tokens, grads, out = refs[:n], refs[n:-1], refs[-1]
        for c in range(0, width, block):
            out[c:c + block] = sum(dot(t[:, c:c + block], g[:, slice(*cut)], 0, 0) for t, g in zip(tokens, grads)).astype(BF)

    return local_call(kernel, [(width, cols)], *tokens, *grads)[0]


def add(*values):
    return sum(v.astype(F32) for v in values).astype(BF)


def cuts_of(size, cuts):
    unit = size // sum(cuts)
    ends = [0]
    for c in cuts:
        ends.append(ends[-1] + c * unit)
    return list(zip(ends[:-1], ends[1:]))


def pick(straight, one, two):
    return jnp.where(straight, one, two), jnp.where(straight, two, one)


def local(tokens, weight, out_grad):
    row, z = lax.axis_index("row"), lax.axis_index("col")
    straight = row // 8 == lax.axis_index("dp")
    x, core = row // 2 % 4, row % 2
    place = jnp.stack([(2 * z - x + 8) % 4, core, *pick(straight, 0, 2)]).astype(jnp.int32)
    t_cuts, f_cuts = cuts_of(tokens.shape[0], TOK_CUTS), cuts_of(weight.shape[1], FF_CUTS)
    step = Steps()
    chunks = ((0, 0), (0, 1), (1, 0), (1, 1))
    w_mate, tok, act, grads = [None] * 2, [None] * 2, {}, {}
    parts, acts, pre = {}, {}, {}

    def project(i):
        t, f = chunks[i]
        parts[i] = forward(*tok[t], weight, w_mate[f], f_cuts[f])
        return reduce_first(parts[i][2], parts[i][3], shift_col)

    def reduce_on(i, up, down):
        return reduce_second(parts[i][1], parts[i][4], up, down, shift_col)

    def activate_on(i, one, two):
        t, f = chunks[i]
        act[t, f], pre[i] = activate(parts[i][0], one, two, out_grad[slice(*t_cuts[t]), slice(*f_cuts[f])])
        return gather_first(pre[i], shift_col)

    def gathered(i, last, following, top, bottom):
        grads[chunks[i]] = jnp.concatenate([pre[i], following, top, bottom, last])

    def back(t, slots, filler=False):
        return token_part(place, [grads[t, f] for f in range(2)], weight, w_mate, f_cuts, slots, filler)

    def weight_back(f, which, part=0, of=1):
        cols = f_cuts[f][1] - f_cuts[f][0]
        middle = (cols // 128 + 1) // 2 * 128
        cut = (0, cols) if of == 1 else ((0, middle), (middle, cols))[part]
        return weight_part([tok[t][which] for t in range(2)], [grads[t, f] for t in range(2)], cut)

    def turn_back(summed):
        width = summed.shape[1] // 2
        same, flipped = pick(straight, summed[:, :width], summed[:, width:])
        return turn_back_z(same, 0), turn_back_z(flipped, 1)

    same, flipped = turn(tokens, 0), turn(tokens, 1)
    same, w_first = step(same, weight[:, slice(*f_cuts[0])])
    flipped, = step(flipped)
    w_mate[0] = swap_dp(w_first)
    block = jnp.concatenate(pick(straight, same, flipped), axis=1)
    b0, b1 = block[slice(*t_cuts[0])], block[slice(*t_cuts[1])]
    last, following = step(*gather_first(b0, shift_x))
    far = gather_second(last, following, shift_x)
    three = jnp.concatenate([b0, following, last])
    mate_three = swap_core(three)
    top, bottom, b1, w_next = step(*far, b1, weight[:, slice(*f_cuts[1])])
    far = jnp.concatenate([top, bottom])
    mate_far = swap_core(far)
    w_mate[1] = swap_dp(w_next)
    mate_far, mate_three, w_mate[0] = step(mate_far, mate_three, w_mate[0])
    tok[0] = join_cores(place, (three, far), (mate_three, mate_far), ((0, 1, 3), (2,)))
    a = project(0)
    b1, _ = step(b1, parts[0][0])
    ring = [b1, shift_x(b1, 1)]
    a = reduce_on(0, *step(*a))
    ring[1], = step(ring[1])
    ring.append(shift_x(ring[1], 1))

    a = activate_on(0, *step(*a))
    ring[2], _ = step(ring[2], pre[0])
    ring.append(shift_x(ring[2], 1))
    w_mate[1], = step(w_mate[1])
    b = project(1)
    a0 = step(*a, parts[1][0])[:2]
    a = gather_second(*a0, shift_col)
    *b, ring[3], top, bottom = step(*b, ring[3], *a)
    b = reduce_on(1, *b)
    line = jnp.concatenate(ring)
    mate = swap_core(line)
    gathered(0, *a0, top, bottom)
    mate, = step(mate)
    tok[1] = join_cores(place, (line,), (mate,), ((0, 3, 2, 1),))
    a = project(2)
    b = activate_on(1, *step(*b, parts[2][0])[:2])
    a = reduce_on(2, *step(*a, pre[1])[:2])
    b0 = step(*b)
    b = gather_second(*b0, shift_col)
    a = activate_on(2, *step(*a))
    gathered(1, *b0, *step(*b, pre[2])[:2])
    b = project(3)
    mine3, theirs = back(0, (3,))
    got3 = swap_core(theirs)
    *b, grads[chunks[1]], _ = step(*b, grads[chunks[1]], theirs)
    b = reduce_on(3, *b)
    mine2, theirs = back(0, (2,))
    got2 = swap_core(theirs)
    *a0, got3, grads[chunks[1]], _ = step(*a, got3, grads[chunks[1]], theirs)
    a = gather_second(*a0, shift_col)
    x_sum = shift_x(add(mine3, got3), 1)
    *b, got2 = step(*b, got2)
    b = activate_on(3, *b)
    mine1, theirs = back(0, (1,))
    got1 = swap_core(theirs)
    *a, x_sum, grads[chunks[1]], _, _ = step(*a, x_sum, grads[chunks[1]], theirs, pre[3])
    gathered(2, *a0, *a)
    x_sum = shift_x(add(mine2, got2, x_sum), 1)
    sent = weight_back(0, 1)
    wgot0 = swap_dp(sent)
    *b0, got1, grads[chunks[2]], _ = step(*b, got1, grads[chunks[2]], sent)
    b = gather_second(*b0, shift_col)
    mine0, theirs = back(0, (0,))
    got0 = swap_core(theirs)
    *b, x_sum, grads[chunks[2]], _ = step(*b, x_sum, grads[chunks[2]], theirs)
    x_sum = shift_x(add(mine1, got1, x_sum), 1)

    gathered(3, *b0, *b)
    mine2, theirs = back(1, (2,))
    got2 = swap_core(theirs)
    grads[chunks[3]], _ = step(grads[chunks[3]], theirs)
    mine, theirs = back(1, (1, 3))
    got = swap_core(theirs)
    got2, grads[chunks[3]], _ = step(got2, grads[chunks[3]], theirs)
    line = add(mine2, got2)
    half = line.shape[0] // 2
    x_first = reduce_first(line[:half], line[half:], shift_x)
    sent = weight_back(1, 1, 0, 2)
    *x_first, got, wgot0, grads[chunks[2]], grads[chunks[3]], sent = step(
        *x_first, got, wgot0, grads[chunks[2]], grads[chunks[3]], sent
    )
    wgot1 = [swap_dp(sent)]
    line = add(mine, got)
    rows = 2 * half
    x_second = reduce_second(line[:rows], line[rows:], *x_first, shift_x)
    mine1, theirs = back(1, (0,))
    got1 = swap_core(theirs)
    sent = weight_back(1, 1, 1, 2)
    keep0 = weight_back(0, 0)
    *x_second, x_sum, got0, got1, wgot1[0], sent, tok_keep, keep0 = step(
        *x_second, x_sum, got0, got1, wgot1[0], sent, tok[1][0], keep0
    )
    wgot1.append(swap_dp(sent))
    sum0, sum1 = add(mine0, got0, x_sum), add(mine1, got1, *x_second)
    same, flipped = turn_back(jnp.concatenate([sum0, sum1]))
    dw_out = [add(keep0, wgot0), None]
    tok[1] = (tok_keep, tok[1][1])
    keep1 = weight_back(1, 0)
    same, flipped, keep1, _ = step(same, flipped, keep1, dw_out[0])
    turned = turn_back_x(same, 0), turn_back_x(flipped, 1)
    wgot1[1], = step(wgot1[1])
    dw_out[1] = add(keep1, jnp.concatenate(wgot1, axis=1))
    dx_out = [add(*step(*turned, dw_out[1])[:2])]
    activated = jnp.concatenate([jnp.concatenate([act[t, f] for f in range(2)], axis=1) for t in range(2)])
    return activated, jnp.concatenate(dx_out), jnp.concatenate(dw_out, axis=1)


def solution(mesh):
    spec = P(("dp", "col"), "row")
    return jax.shard_map(local, mesh=mesh, in_specs=(spec,) * 3, out_specs=(spec,) * 3, check_vma=False)
```

```python
import jax
import jax.numpy as jnp
from jax import lax
from jax.experimental import pallas as pl
from jax.experimental.pallas import tpu as pltpu
from jax.sharding import PartitionSpec as P

BF, F32 = jnp.bfloat16, jnp.float32
TOK_CUTS = (1, 1)
FF_CUTS = (1, 1)
VMEM = pl.BlockSpec(memory_space=pltpu.VMEM)
SMEM = pl.BlockSpec(memory_space=pltpu.SMEM)


class Steps:
    def __init__(self):
        self.mark = None

    def __call__(self, *values):
        held = values if self.mark is None else (*values, self.mark)
        held = lax.optimization_barrier(held)
        self.mark = held[0]
        return held[: len(values)]


def swap_dp(value):
    return lax.ppermute(value, "dp", [(0, 1), (1, 0)])


def shift_col(value, step):
    return lax.ppermute(value, "col", [(i, (i + step) % 4) for i in range(4)])


def row_of(high, along_x, core):
    return (high * 4 + along_x) * 2 + core


def shift_x(value, step):
    pairs = [
        (row_of(h, x, c), row_of(h, (x + step) % 4, c))
        for h in range(2) for x in range(4) for c in range(2)
    ]
    return lax.ppermute(value, "row", pairs)


def swap_core(value):
    return lax.ppermute(value, "row", [(i, i ^ 1) for i in range(16)])


def move(value, target):
    pairs = []
    for high in range(2):
        for along_x in range(4):
            for core in range(2):
                for z in range(4):
                    to_high, to_x, to_z = target(high, along_x, z)
                    pairs.append((row_of(high, along_x, core) * 4 + z, row_of(to_high, to_x % 4, core) * 4 + to_z % 4))
    return lax.ppermute(value, ("row", "col"), pairs)


def turn(value, flip):
    return move(value, lambda h, x, z: (h ^ flip, x + z + 2 * flip, x))


def turn_back_z(value, flip):
    return move(value, lambda h, x, z: (h, x, x - z + 2 * flip))


def turn_back_x(value, flip):
    return move(value, lambda h, x, z: (h ^ flip, x - z + 2 * flip, z))


def gather_first(own, shift):
    return shift(own, 1), shift(own, -1)


def gather_second(last, following, shift):
    half = last.shape[0] // 2
    return shift(last[:half], 1), shift(following[half:], -1)


def reduce_first(top, bottom, shift):
    return shift(top, 1), shift(bottom, -1)


def reduce_second(following, last, up, down, shift):
    half = up.shape[0]
    following = jnp.concatenate([(following[:half].astype(F32) + up.astype(F32)).astype(BF), following[half:]])
    last = jnp.concatenate([last[:half], (last[half:].astype(F32) + down.astype(F32)).astype(BF)])
    return shift(following, 1), shift(last, -1)


def local_call(kernel, shapes, *args, scalars=0, flops=0):
    return pl.pallas_call(
        kernel,
        in_specs=[SMEM] * scalars + [VMEM] * (len(args) - scalars),
        out_specs=[VMEM] * len(shapes),
        out_shape=[jax.ShapeDtypeStruct(s, BF) for s in shapes],
        compiler_params=pltpu.CompilerParams(vmem_limit_bytes=12 * 2**20),
        cost_estimate=pl.CostEstimate(flops=flops, bytes_accessed=0, transcendentals=0),
    )(*args)


def dot(a, b, over_a, over_b):
    return lax.dot_general(a, b, (((over_a,), (over_b,)), ((), ())), preferred_element_type=F32)


def join_cores(place, lines, mates, slots):
    rows, width = sum(v.shape[0] for v in lines) // 4, lines[0].shape[1]
    side, n = width // 2, len(lines)

    def kernel(place, *refs):
        own, other = refs[-2:]
        first = place[1] == 0
        for line, mate, held in zip(refs[:n], refs[n:-2], slots):
            for i, slot in enumerate(held):
                at = slice(i * rows, (i + 1) * rows)
                mine, theirs = line[at], mate[at]
                left, right = jnp.where(first, mine, theirs), jnp.where(first, theirs, mine)
                for out, turned, cols in ((own, place[2], slice(0, side)), (other, place[3], slice(side, width))):
                    to = pl.ds(pl.multiple_of((slot + turned - place[0] + 4) % 4 * rows, rows), rows)
                    out[to, :side], out[to, side:] = left[:, cols], right[:, cols]

    return local_call(kernel, [(4 * rows, width)] * 2, place, *lines, *mates, scalars=1)


def forward(own, other, w_own, w_mate, cut):
    rows, cols = own.shape[0] // 4, cut[1] - cut[0]
    half = rows // 2

    def kernel(own, other, w_own, w_mate, zero, one, top, bottom, three):
        left, right = w_own[:, slice(*cut)], w_mate[...]
        for k in (2, 1, 3, 0):
            at = slice(k * rows, (k + 1) * rows)
            share = (dot(own[at], left, 1, 0) + dot(other[at], right, 1, 0)).astype(BF)
            if k == 2:
                top[...], bottom[...] = share[:half], share[half:]
            else:
                (zero, one, None, three)[k][...] = share

    full, part = (rows, cols), (half, cols)
    return local_call(kernel, [full, full, part, part, full], own, other, w_own, w_mate)


def activate(share, from_last, from_following, out_grad):
    def kernel(share, one, two, out_grad, activated, pre_grad):
        rows = 32
        for r in range(0, share.shape[0], rows):
            at = slice(r, r + rows)
            v = share[at].astype(F32) + one[at].astype(F32) + two[at].astype(F32)
            scale, cubic = 0.7978845608028654, 0.044715
            square = v * v
            tanh = jnp.tanh(scale * (v + cubic * (v * square)))
            gate = 0.5 * (1.0 + tanh)
            activated[at] = (v * gate).astype(BF)
            slope = gate + 0.5 * v * (1.0 - tanh * tanh) * (scale * (1.0 + 3.0 * cubic * square))
            pre_grad[at] = (out_grad[at].astype(F32) * slope).astype(BF)

    return local_call(kernel, [share.shape] * 2, share, from_last, from_following, out_grad)


def token_part(place, grads, w_own, w_mates, cuts, slots, filler):
    rows, width = grads[0].shape[0] // 4, w_own.shape[0]
    side, n = width // 2, len(grads)

    def kernel(place, *refs):
        grads, w_own, w_mates, mine, theirs = refs[:n], refs[n], refs[n + 1:-2], refs[-2], refs[-1]
        for i, slot in enumerate(slots):
            at, at_other = (pl.ds(pl.multiple_of((slot + s - place[0] + 4) % 4 * rows, rows), rows) for s in (place[2], place[3]))
            own = sum(dot(g[at], w_own[:, slice(*cut)], 1, 1) for g, cut in zip(grads, cuts)).astype(BF)
            other = sum(dot(g[at_other], w[...], 1, 1) for g, w in zip(grads, w_mates)).astype(BF)
            zero = jnp.concatenate([own[:, :side], other[:, :side]], axis=1)
            one = jnp.concatenate([own[:, side:], other[:, side:]], axis=1)
            first = place[1] == 0
            to = slice(i * rows, (i + 1) * rows)
            mine[to], theirs[to] = jnp.where(first, zero, one), jnp.where(first, one, zero)

    shape = (len(slots) * rows, width)
    flops = 4 * shape[0] * w_own.size if filler else 0
    return local_call(kernel, [shape, shape], place, *grads, w_own, *w_mates, scalars=1, flops=flops)


def weight_part(tokens, grads, cut):
    n, width, cols = len(tokens), tokens[0].shape[1], cut[1] - cut[0]
    block = min(256, width)

    def kernel(*refs):
        tokens, grads, out = refs[:n], refs[n:-1], refs[-1]
        for c in range(0, width, block):
            out[c:c + block] = sum(dot(t[:, c:c + block], g[:, slice(*cut)], 0, 0) for t, g in zip(tokens, grads)).astype(BF)

    return local_call(kernel, [(width, cols)], *tokens, *grads)[0]


def add(*values):
    return sum(v.astype(F32) for v in values).astype(BF)


def cuts_of(size, cuts):
    unit = size // sum(cuts)
    ends = [0]
    for c in cuts:
        ends.append(ends[-1] + c * unit)
    return list(zip(ends[:-1], ends[1:]))


def pick(straight, one, two):
    return jnp.where(straight, one, two), jnp.where(straight, two, one)


def local(tokens, weight, out_grad):
    row, z = lax.axis_index("row"), lax.axis_index("col")
    straight = row // 8 == lax.axis_index("dp")
    x, core = row // 2 % 4, row % 2
    place = jnp.stack([(2 * z - x + 8) % 4, core, *pick(straight, 0, 2)]).astype(jnp.int32)
    t_cuts, f_cuts = cuts_of(tokens.shape[0], TOK_CUTS), cuts_of(weight.shape[1], FF_CUTS)
    step = Steps()
    chunks = ((0, 0), (0, 1), (1, 0), (1, 1))
    w_mate, tok, act, grads = [None] * 2, [None] * 2, {}, {}
    parts, acts, pre = {}, {}, {}

    def project(i):
        t, f = chunks[i]
        parts[i] = forward(*tok[t], weight, w_mate[f], f_cuts[f])
        return reduce_first(parts[i][2], parts[i][3], shift_col)

    def reduce_on(i, up, down):
        return reduce_second(parts[i][1], parts[i][4], up, down, shift_col)

    def activate_on(i, one, two):
        t, f = chunks[i]
        act[t, f], pre[i] = activate(parts[i][0], one, two, out_grad[slice(*t_cuts[t]), slice(*f_cuts[f])])
        return gather_first(pre[i], shift_col)

    def gathered(i, last, following, top, bottom):
        grads[chunks[i]] = jnp.concatenate([pre[i], following, top, bottom, last])

    def back(t, slots, filler=False):
        return token_part(place, [grads[t, f] for f in range(2)], weight, w_mate, f_cuts, slots, filler)

    def weight_back(f, which, part=0, of=1):
        cols = f_cuts[f][1] - f_cuts[f][0]
        middle = (cols // 128 + 1) // 2 * 128
        cut = (0, cols) if of == 1 else ((0, middle), (middle, cols))[part]
        return weight_part([tok[t][which] for t in range(2)], [grads[t, f] for t in range(2)], cut)

    def turn_back(summed):
        width = summed.shape[1] // 2
        same, flipped = pick(straight, summed[:, :width], summed[:, width:])
        return turn_back_z(same, 0), turn_back_z(flipped, 1)

    same, flipped = turn(tokens, 0), turn(tokens, 1)
    same, w_first = step(same, weight[:, slice(*f_cuts[0])])
    flipped, = step(flipped)
    w_mate[0] = swap_dp(w_first)
    block = jnp.concatenate(pick(straight, same, flipped), axis=1)
    b0, b1 = block[slice(*t_cuts[0])], block[slice(*t_cuts[1])]
    last, following = step(*gather_first(b0, shift_x))
    far = gather_second(last, following, shift_x)
    three = jnp.concatenate([b0, following, last])
    mate_three = swap_core(three)
    top, bottom, b1, w_next = step(*far, b1, weight[:, slice(*f_cuts[1])])
    far = jnp.concatenate([top, bottom])
    mate_far = swap_core(far)
    w_mate[1] = swap_dp(w_next)
    mate_far, mate_three, w_mate[0] = step(mate_far, mate_three, w_mate[0])
    tok[0] = join_cores(place, (three, far), (mate_three, mate_far), ((0, 1, 3), (2,)))
    a = project(0)
    b1, _ = step(b1, parts[0][0])
    ring = [b1, shift_x(b1, 1)]
    a = reduce_on(0, *step(*a))
    ring[1], = step(ring[1])
    ring.append(shift_x(ring[1], 1))

    a = activate_on(0, *step(*a))
    ring[2], _ = step(ring[2], pre[0])
    ring.append(shift_x(ring[2], 1))
    w_mate[1], = step(w_mate[1])
    b = project(1)
    a0 = step(*a, parts[1][0])[:2]
    a = gather_second(*a0, shift_col)
    *b, ring[3], top, bottom = step(*b, ring[3], *a)
    b = reduce_on(1, *b)
    line = jnp.concatenate(ring)
    mate = swap_core(line)
    gathered(0, *a0, top, bottom)
    mate, = step(mate)
    tok[1] = join_cores(place, (line,), (mate,), ((0, 3, 2, 1),))
    a = project(2)
    b = activate_on(1, *step(*b, parts[2][0])[:2])
    a = reduce_on(2, *step(*a, pre[1])[:2])
    b0 = step(*b)
    b = gather_second(*b0, shift_col)
    a = activate_on(2, *step(*a))
    gathered(1, *b0, *step(*b, pre[2])[:2])
    b = project(3)
    mine3, theirs = back(0, (3,))
    got3 = swap_core(theirs)
    *b, grads[chunks[1]] = step(*b, grads[chunks[1]])
    b = reduce_on(3, *b)
    mine2, theirs = back(0, (2,))
    got2 = swap_core(theirs)
    *a0, got3, grads[chunks[1]], _ = step(*a, got3, grads[chunks[1]], theirs)
    a = gather_second(*a0, shift_col)
    x_sum = shift_x(add(mine3, got3), 1)
    *b, got2 = step(*b, got2)
    b = activate_on(3, *b)
    mine1, theirs = back(0, (1,))
    got1 = swap_core(theirs)
    *a, x_sum, grads[chunks[1]], _, _ = step(*a, x_sum, grads[chunks[1]], theirs, pre[3])
    gathered(2, *a0, *a)
    x_sum = shift_x(add(mine2, got2, x_sum), 1)
    sent = weight_back(0, 1)
    wgot0 = swap_dp(sent)
    *b0, got1, grads[chunks[2]], _ = step(*b, got1, grads[chunks[2]], sent)
    b = gather_second(*b0, shift_col)
    mine0, theirs = back(0, (0,))
    got0 = swap_core(theirs)
    *b, x_sum, grads[chunks[2]], _ = step(*b, x_sum, grads[chunks[2]], theirs)
    x_sum = shift_x(add(mine1, got1, x_sum), 1)

    gathered(3, *b0, *b)
    mine2, theirs = back(1, (2,))
    got2 = swap_core(theirs)
    grads[chunks[3]], _ = step(grads[chunks[3]], theirs)
    mine, theirs = back(1, (1, 3))
    got = swap_core(theirs)
    got2, grads[chunks[3]], _ = step(got2, grads[chunks[3]], theirs)
    line = add(mine2, got2)
    half = line.shape[0] // 2
    x_first = reduce_first(line[:half], line[half:], shift_x)
    sent = weight_back(1, 1, 0, 2)
    *x_first, got, wgot0, grads[chunks[2]], grads[chunks[3]], sent = step(
        *x_first, got, wgot0, grads[chunks[2]], grads[chunks[3]], sent
    )
    wgot1 = [swap_dp(sent)]
    line = add(mine, got)
    rows = 2 * half
    x_second = reduce_second(line[:rows], line[rows:], *x_first, shift_x)
    mine1, theirs = back(1, (0,))
    got1 = swap_core(theirs)
    sent = weight_back(1, 1, 1, 2)
    keep0 = weight_back(0, 0)
    *x_second, x_sum, got0, got1, wgot1[0], sent, tok_keep, keep0 = step(
        *x_second, x_sum, got0, got1, wgot1[0], sent, tok[1][0], keep0
    )
    wgot1.append(swap_dp(sent))
    sum0, sum1 = add(mine0, got0, x_sum), add(mine1, got1, *x_second)
    same, flipped = turn_back(jnp.concatenate([sum0, sum1]))
    dw_out = lax.dynamic_update_slice(jnp.zeros(weight.shape, BF), add(keep0, wgot0), (0, 0))
    tok[1] = (tok_keep, tok[1][1])
    keep1 = weight_back(1, 0)
    same, flipped, keep1, wgot1[0], dw_out = step(same, flipped, keep1, wgot1[0], dw_out)
    turned = turn_back_x(same, 0), turn_back_x(flipped, 1)
    start, middle = f_cuts[1][0], wgot1[0].shape[1]
    dw_out = lax.dynamic_update_slice(dw_out, add(keep1[:, :middle], wgot1[0]), (0, start))
    wgot1[1], dw_out = step(wgot1[1], dw_out)
    dw_out = lax.dynamic_update_slice(dw_out, add(keep1[:, middle:], wgot1[1]), (0, start + middle))
    dx_out = [add(*step(*turned))]
    activated = jnp.concatenate([jnp.concatenate([act[t, f] for f in range(2)], axis=1) for t in range(2)])
    return activated, jnp.concatenate(dx_out), dw_out


def solution(mesh):
    spec = P(("dp", "col"), "row")
    return jax.shard_map(local, mesh=mesh, in_specs=(spec,) * 3, out_specs=(spec,) * 3, check_vma=False)
```
